256 devices in a mesh: hist: 32 (over z, y), orow: 2 (over x_lo), ocol: 4 (over x_hi, core).
Axes of the slice: x: 4 (x_hi: 2, x_lo: 2; x = x_hi * 2 + x_lo), y: 4, z: 8, core: 2. Of those that a mesh axis runs over, the one named last changes fastest.
Arguments:
- lesser_hist: float32 [2, 128, 256, 256], P(None, 'hist', 'ocol', 'orow'), may hold values from -6 to 6
- greater_hist: float32 [2, 128, 256, 256], P(None, 'hist', 'orow', 'ocol'), may hold values from -6 to 6
- advanced_hist: float32 [2, 128, 32, 256, 256], P(None, 'hist', 'ocol', None, 'orow'), may hold values from -6 to 6
- current_row: float32 [2, 32, 256, 256], P(None, 'ocol', 'hist', 'orow'), may hold values from -6 to 6
- adjacency: int32 [256, 256], P('hist'), may hold values from 0 to 1, as said below
- weight_table: int32 [128], P('hist'), may hold values from 1 to 48
- step_index: int32 [1], replicated, may hold values from 32 to 127
Outputs:
- new_row: float32 [2, 32, 256, 256], P(None, 'ocol', 'hist', 'orow')
The draws below stay inside these ranges and needn't reach their ends.
Inputs may be any that keep to these rules, and one draw needn't show every extreme that they name: `adjacency`: symmetric, zero on the diagonal.
All inputs are finite; a program needn't handle non-finite values.
Results may differ from the reference program's by a relative error of at most 0.0001.
Values sent between devices are 32-bit elements; how exact they have to be, the bound alone decides.
A program may use at most 64 MiB of HBM per device.

```python
import jax
import jax.numpy as jnp
from jax import lax

NORB = 256
TPRIME = 32
SLICES = 128


def draw_adjacency(key, part):
    key = jax.random.fold_in(key, 7)
    draws = jax.random.randint(key, (NORB, NORB), 0, NORB)
    upper = jnp.triu((draws < 3).astype(jnp.int32), 1)
    return upper + upper.T


def with_ends(result, stream_key, low, largest):
    place = [jax.random.randint(jax.random.fold_in(stream_key, axis), (), 0, length) for axis, length in enumerate(result.shape)]
    widest = result.shape.index(max(result.shape))
    beside = place[:widest] + [(place[widest] + 1) % result.shape[widest]] + place[widest + 1:]
    return result.at[tuple(place)].set(low).at[tuple(beside)].set(largest)


def steps_of(rng, shape, pieces, low, top_value):
    def one(dim, parts):
        steps = jax.random.uniform(jax.random.fold_in(jax.random.fold_in(rng, 6), dim), (parts,), jnp.float32, low / len(pieces), top_value / len(pieces))
        return jnp.repeat(jnp.exp(steps), shape[dim] // parts).reshape((-1,) + (1,) * (len(shape) - dim - 1))

    gain = one(*pieces[0])
    for cut in pieces[1:]:
        gain = gain * one(*cut)
    return gain


def gaussian(rng, extent, spread, reach, shards=(), kind=jnp.bfloat16):
    values = jax.random.normal(rng, extent, jnp.float32) * spread
    if len(shards) > 0:
        values = steps_of(rng, extent, shards, -0.22, 0.18) * values
    return jnp.clip(values, min=-reach, max=reach).astype(kind)


def setup_inputs(seed: int = 0) -> dict:
    arg_keys = jax.random.split(jax.random.key(seed), 8)
    return {
        "lesser_hist": gaussian(arg_keys[0], (2, SLICES, NORB, NORB), 1.0, 6.0, ((1, 32), (2, 4), (3, 2)), jnp.float32),
        "greater_hist": gaussian(arg_keys[1], (2, SLICES, NORB, NORB), 1.0, 6.0, ((1, 32), (2, 2), (3, 4)), jnp.float32),
        "advanced_hist": gaussian(arg_keys[2], (2, SLICES, TPRIME, NORB, NORB), 1.0, 6.0, ((1, 32), (2, 4), (4, 2)), jnp.float32),
        "current_row": gaussian(arg_keys[3], (2, TPRIME, NORB, NORB), 1.0, 6.0, ((1, 4), (2, 32), (3, 2)), jnp.float32),
        "adjacency": draw_adjacency(jax.random.fold_in(arg_keys[7], 71), 0),
        "weight_table": with_ends(jax.random.randint(arg_keys[5], (SLICES,), 1, 49), jax.random.fold_in(arg_keys[5], 1), 1, 48).astype(jnp.int32),
        "step_index": jax.random.randint(arg_keys[6], (1,), SLICES // 4, SLICES).astype(jnp.int32),
    }


coupling_square = 0.25
hopping = 4.0
time_step = 0.01


def self_energy(lesser, greater_t):
    lesser_re, lesser_im = lesser[0], lesser[1]
    greater_re, greater_im = greater_t[0], greater_t[1]
    square_re = lesser_re * lesser_re - lesser_im * lesser_im
    square_im = 2.0 * lesser_re * lesser_im
    sigma_re = coupling_square * (square_re * greater_re - square_im * greater_im)
    sigma_im = coupling_square * (square_re * greater_im + square_im * greater_re)
    return jnp.stack([sigma_re, sigma_im])


def slice_term(sigma_one, history_one):
    combos = jnp.einsum('cik,dtkj->cdtij', sigma_one, history_one, precision=lax.Precision.HIGHEST, preferred_element_type=jnp.float32)
    return jnp.stack([combos[0, 0] - combos[1, 1], combos[0, 1] + combos[1, 0]])


def reference(lesser_hist, greater_hist, advanced_hist, current_row, adjacency, weight_table, step_index):
    sigma = self_energy(lesser_hist, jnp.swapaxes(greater_hist, 2, 3))
    slot_ids = jnp.arange(SLICES, dtype=jnp.int32)
    weights = jnp.where(slot_ids <= step_index[0], weight_table.astype(jnp.float32) / 24.0, jnp.float32(0.0))
    sigma_w = sigma * weights[None, :, None, None]

    def add_slice(position, accumulated):
        sigma_one = lax.dynamic_index_in_dim(sigma_w, position, 1, keepdims=False)
        history_one = lax.dynamic_index_in_dim(advanced_hist, position, 1, keepdims=False)
        return accumulated + slice_term(sigma_one, history_one)

    start = jnp.zeros((2, TPRIME, NORB, NORB), jnp.float32)
    collision = lax.fori_loop(0, SLICES, add_slice, start)
    hop_matrix = -hopping * adjacency.astype(jnp.float32)
    hop_term = jnp.einsum('ik,ctkj->ctij', hop_matrix, current_row, precision=lax.Precision.HIGHEST, preferred_element_type=jnp.float32)
    summed = collision + hop_term
    return jnp.stack([current_row[0] + time_step * summed[1], current_row[1] - time_step * summed[0]])
```

```python
import jax
import jax.numpy as jnp
from jax import lax
from jax.sharding import PartitionSpec as P

coupling_square = 0.25
hopping = 4.0
time_step = 0.01


def self_energy(lesser, greater_t):
    lesser_re, lesser_im = (lesser[0], lesser[1])
    greater_re, greater_im = (greater_t[0], greater_t[1])
    square_re = lesser_re * lesser_re - lesser_im * lesser_im
    square_im = 2.0 * lesser_re * lesser_im
    sigma_re = coupling_square * (square_re * greater_re - square_im * greater_im)
    sigma_im = coupling_square * (square_re * greater_im + square_im * greater_re)
    return jnp.stack([sigma_re, sigma_im])


def on_device(
    lesser_hist, greater_hist, advanced_hist, current_row, adjacency, weight_table, step_index
):
    slices_here = lesser_hist.shape[1]
    slot_ids = lax.axis_index("hist") * slices_here + lax.iota(jnp.int32, slices_here)
    weights = jnp.where(
        slot_ids <= step_index[0], weight_table.astype(jnp.float32) / 24.0, jnp.float32(0.0)
    )
    sigma = self_energy(lesser_hist, jnp.swapaxes(greater_hist, 2, 3))
    sigma = sigma * weights[None, :, None, None]
    sigma = lax.all_gather(sigma, "ocol", axis=2, tiled=True)
    sigma = lax.all_gather(sigma, "orow", axis=3, tiled=True)
    combos = jnp.einsum(
        "csik,dstkj->cdtij",
        sigma,
        advanced_hist,
        precision=lax.Precision.HIGH,
        preferred_element_type=jnp.float32,
    )
    collision = jnp.stack([combos[0, 0] - combos[1, 1], combos[0, 1] + combos[1, 0]])
    hop = jnp.einsum(
        "ki,ctkj->ctij",
        -hopping * adjacency.astype(jnp.float32),
        current_row,
        precision=lax.Precision.HIGHEST,
        preferred_element_type=jnp.float32,
    )
    summed = lax.psum_scatter(collision + hop, "hist", scatter_dimension=2, tiled=True)
    return jnp.stack(
        [current_row[0] + time_step * summed[1], current_row[1] - time_step * summed[0]]
    )


def solution(mesh):
    in_specs = (
        P(None, "hist", "ocol", "orow"),
        P(None, "hist", "orow", "ocol"),
        P(None, "hist", "ocol", None, "orow"),
        P(None, "ocol", "hist", "orow"),
        P("hist", None),
        P("hist"),
        P(),
    )
    out_specs = P(None, "ocol", "hist", "orow")
    return jax.shard_map(
        on_device, mesh=mesh, in_specs=in_specs, out_specs=out_specs, check_vma=False
    )
```

```python
import functools

import jax
import jax.numpy as jnp
from jax import lax
from jax.experimental import pallas as pl
from jax.experimental.pallas import tpu as pltpu
from jax.sharding import PartitionSpec as P

coupling_square = 0.25
hopping = 4.0
time_step = 0.01

NZ, NY = 8, 4
NS, NT = 4, 8
ROWS, COLS = 64, 128
HALVES = 2
RB = ROWS // HALVES
NZZ = NZ // HALVES
STAGES = ((0, 0, 4), (0, 4, 4), (1, 0, 4), (1, 4, 4))
MESH = pl.DeviceIdType.MESH
f32, bf16 = jnp.float32, jnp.bfloat16


def split(x):
    hi = x.astype(bf16)
    return hi, (x - hi.astype(f32)).astype(bf16)


def kernel(
    table, step, lesser, greater, advanced, row, adjacency, out,
    les_b, gre_b, adv_b, row_b, adj_b, gath, lhs_hi, lhs_lo, rhs_hi, rhs_lo, hop_l, hop_r,
    in_sem, adv_sem, gs, gr, ys, yr, zs, zr, *bufs,
):
    n_st = len(STAGES)
    part, y1, y2, zb = (bufs[i * n_st : (i + 1) * n_st] for i in range(4))
    h, r, c = (lax.axis_index(a) for a in ("hist", "orow", "ocol"))
    z, y = lax.div(h, NY), lax.rem(h, NY)
    x, k = lax.div(c, 2) * 2 + r, lax.rem(c, 2)

    def wrap(v, n):
        return lax.rem(v + n, n)

    def dev(dx=0, dy=0, dz=0, other=False):
        xx = wrap(x + dx, 4)
        kk = 1 - k if other else k
        hh = wrap(z + dz, NZ) * NY + wrap(y + dy, NY)
        return (hh, lax.rem(xx, 2), lax.div(xx, 2) * 2 + kk)

    def remote(src, dst, ss, rs, to):
        return pltpu.make_async_remote_copy(
            src_ref=src, dst_ref=dst, send_sem=ss, recv_sem=rs, device_id=to, device_id_type=MESH
        )

    inputs = [
        pltpu.make_async_copy(a, b, in_sem.at[i])
        for i, (a, b) in enumerate(
            ((lesser, les_b), (greater, gre_b), (row, row_b), (adjacency, adj_b))
        )
    ]
    for copy in inputs:
        copy.start()
    adv = [pltpu.make_async_copy(advanced.at[:, :, t], adv_b.at[t], adv_sem.at[t]) for t in range(NT)]
    for copy in adv:
        copy.start()

    barrier = pltpu.get_barrier_semaphore()
    friends = [dev(dx=1), dev(dx=-1), dev(other=True), dev(dy=1), dev(dy=-1)]
    friends += [dev(dz=d) for d in range(1, NZ)]
    for friend in friends:
        pl.semaphore_signal(barrier, inc=1, device_id=friend, device_id_type=MESH)

    inputs[0].wait()
    inputs[1].wait()
    for s in range(NS):
        used = h * NS + s <= step[0]
        scale = jnp.where(used, table[s], 0).astype(f32) * (coupling_square / 24.0)
        lr, li = les_b[0, s], les_b[1, s]
        gre, gim = gre_b[0, s].T, gre_b[1, s].T
        sr = (lr * lr - li * li) * scale
        si = (2.0 * lr * li) * scale
        re = sr * gre - si * gim
        im = sr * gim + si * gre
        for hf in range(HALVES):
            gath[hf, 0, s, 0] = re[hf * RB : (hf + 1) * RB]
            gath[hf, 0, s, 1] = im[hf * RB : (hf + 1) * RB]

    pl.semaphore_wait(barrier, len(friends))

    slot_of = {0: (0, False), 1: (0, True), 2: (-1, False), 3: (-1, True),
               4: (1, False), 5: (1, True), 6: (2, False), 7: (2, True)}
    lo_s, hi_s, all_s = pl.ds(0, 2), pl.ds(2, 2), pl.ds(0, 4)

    def piece(hf, n, src_slot, dst_slot, ss, to):
        return remote(
            gath.at[hf, src_slot, ss], gath.at[hf, dst_slot, ss], gs.at[hf, n], gr.at[hf, n], to
        )

    right, left, twin = dev(dx=1), dev(dx=-1), dev(other=True)
    g = [
        [
            piece(hf, 0, 0, 2, lo_s, right),
            piece(hf, 1, 0, 4, hi_s, left),
            piece(hf, 2, 0, 2, hi_s, right),
            piece(hf, 3, 0, 4, lo_s, left),
            piece(hf, 4, 0, 1, all_s, twin),
            piece(hf, 5, 2, 6, lo_s, right),
            piece(hf, 6, 4, 6, hi_s, left),
            piece(hf, 7, 2, 3, lo_s, twin),
            piece(hf, 8, 4, 5, hi_s, twin),
            piece(hf, 9, 2, 3, hi_s, twin),
            piece(hf, 10, 4, 5, lo_s, twin),
            piece(hf, 11, 6, 7, lo_s, twin),
            piece(hf, 12, 6, 7, hi_s, twin),
        ]
        for hf in range(HALVES)
    ]

    def to_lhs(hf, slot, s_range):
        dx, other = slot_of[slot]
        xx = wrap(x + dx, 4)
        kh = dx % 2
        block = lax.div(xx, 2) * 2 + (1 - k if other else k)
        for s in s_range:
            for cc in range(2):
                hi, lo = split(gath[hf, slot, s, cc])
                lhs_hi[hf, kh, s, cc, block] = hi
                lhs_lo[hf, kh, s, cc, block] = lo

    def begin(hf, names):
        for n in names:
            g[hf][n].start()

    def arrived(hf, names):
        for n in names:
            g[hf][n].wait_recv()

    def to_rhs(first, count):
        def one(t, carry):
            for s in range(NS):
                for cc in range(2):
                    for kh in range(2):
                        half = wrap(r + kh, 2)
                        rows = pl.ds(pl.multiple_of(half * 128, 128), 128)
                        hi, lo = split(adv_b[t, cc, s, rows, :])
                        rhs_hi[t, s, kh * 128 : (kh + 1) * 128, cc * 128 : (cc + 1) * 128] = hi
                        rhs_lo[t, s, kh * 128 : (kh + 1) * 128, cc * 128 : (cc + 1) * 128] = lo
            return carry

        for t in range(first, first + count):
            adv[t].wait()
        lax.fori_loop(first, first + count, one, 0)

    begin(0, (0, 1, 2, 3, 4))
    if HALVES > 1:
        begin(1, (0, 1))

    inputs[2].wait()
    inputs[3].wait()
    adj = adj_b[...].astype(f32) * -hopping
    adj_t = jnp.concatenate([adj, adj, jnp.zeros((112, 256), f32)], axis=0).T.astype(bf16)
    for hf in range(HALVES):
        for b in range(4):
            first = b * ROWS + hf * RB
            hop_l[hf, b * RB : (b + 1) * RB, :] = adj_t[first : first + RB]
    for t in range(NT):
        both = jnp.concatenate([row_b[0, t], row_b[1, t]], axis=1)
        hi = both.astype(bf16).astype(f32)
        full = jnp.concatenate([hi, both - hi, jnp.zeros((112, 256), f32)], axis=0)
        hop_r[t] = full.astype(bf16)

    to_lhs(0, 0, range(NS))
    to_rhs(0, 4)

    def gather_rest(hf, step_n):
        if step_n == 0:
            arrived(hf, (0, 1))
            begin(hf, (5, 6, 7, 8))
        elif step_n == 1:
            arrived(hf, (2, 3))
            begin(hf, (9, 10))
            to_lhs(hf, 2, range(NS))
            to_lhs(hf, 4, range(NS))
            arrived(hf, (4,))
            to_lhs(hf, 1, range(NS))
        elif step_n == 2:
            arrived(hf, (5, 6))
            begin(hf, (11, 12))
            to_lhs(hf, 6, range(NS))
            arrived(hf, (7, 8, 9, 10))
            to_lhs(hf, 3, range(NS))
            to_lhs(hf, 5, range(NS))
        else:
            arrived(hf, (11, 12))
            to_lhs(hf, 7, range(NS))

    gather_rest(0, 0)
    if HALVES > 1:
        begin(1, (2, 3, 4))
        to_lhs(1, 0, range(NS))
    to_rhs(4, 4)
    gather_rest(0, 1)
    if HALVES > 1:
        gather_rest(1, 0)
    gather_rest(0, 2)
    gather_rest(0, 3)

    half = NZZ // 2
    first_h, second_h = pl.ds(0, half), pl.ds(half, half)

    def y_copies(st):
        p = part[st]
        up, down = dev(dy=1), dev(dy=-1)
        ring = [
            (p.at[wrap(y + 2, NY), first_h], y1[st].at[0], up),
            (p.at[wrap(y + 2, NY), second_h], y1[st].at[1], down),
            (p.at[wrap(y + 1, NY), second_h], y2[st].at[0, second_h], up),
            (p.at[wrap(y - 1, NY), first_h], y2[st].at[1, first_h], down),
            (p.at[wrap(y + 1, NY), first_h], y2[st].at[0, first_h], up),
            (p.at[wrap(y - 1, NY), second_h], y2[st].at[1, second_h], down),
        ]
        return [remote(a, b, ys.at[st, i], yr.at[st, i], to) for i, (a, b, to) in enumerate(ring)]

    def z_copy(st, d):
        zz = lax.div(wrap(z + d, NZ), HALVES)
        return remote(part[st].at[y, zz], zb[st].at[d - 1], zs.at[st, d - 1], zr.at[st, d - 1], dev(dz=d))

    def z_each(st, act):
        hf = STAGES[st][0]
        for d in range(1, NZ):
            if HALVES == 1:
                act(z_copy(st, d))
            else:
                @pl.when(lax.rem(z + d, HALVES) == hf)
                def _():
                    act(z_copy(st, d))

    def compute(st):
        hf, t0, nt = STAGES[st]

        def one(t, carry):
            tt = t0 + t
            acc = None
            for s in range(NS):
                def left_of(ref):
                    a = [ref[hf, kh, s].reshape(8 * RB, 128) for kh in range(2)]
                    return jnp.concatenate(a, axis=1)

                a_hi, a_lo = left_of(lhs_hi), left_of(lhs_lo)
                b_hi, b_lo = rhs_hi[tt, s], rhs_lo[tt, s]
                for a, b in ((a_hi, b_hi), (a_hi, b_lo), (a_lo, b_hi)):
                    term = jnp.dot(a, b, preferred_element_type=f32)
                    acc = term if acc is None else acc + term
            hop = jnp.dot(hop_l[hf], hop_r[tt], preferred_element_type=f32)
            m = 4 * RB
            re = acc[:m, :128] - acc[m:, 128:] + hop[:, :128]
            im = acc[:m, 128:] + acc[m:, :128] + hop[:, 128:]
            re, im = (v.reshape(NZZ, NY, 8, 128) for v in (re, im))
            for yy in range(NY):
                part[st][yy, :, 0, t] = re[:, yy]
                part[st][yy, :, 1, t] = im[:, yy]
            return carry

        lax.fori_loop(0, nt, one, 0)
        for copy in y_copies(st)[:4]:
            copy.start()

    def y_late(st):
        copies = y_copies(st)
        copies[0].wait_recv()
        up = wrap(y + 1, NY)
        part[st][up, :half] = part[st][up, :half] + y1[st][0]
        copies[4].start()
        copies[1].wait_recv()
        down = wrap(y - 1, NY)
        part[st][down, half:] = part[st][down, half:] + y1[st][1]
        copies[5].start()

    def z_send(st):
        for copy in y_copies(st)[2:]:
            copy.wait_recv()
        part[st][y] = part[st][y] + y2[st][0] + y2[st][1]
        z_each(st, lambda copy: copy.start())

    def finish(st):
        hf, t0, nt = STAGES[st]

        def receive():
            total = part[st][y, lax.div(z, HALVES)]
            for d in range(1, NZ):
                z_copy(st, d).wait_recv()
                total = total + zb[st][d - 1]
            out[0, t0 : t0 + nt] = row_b[0, t0 : t0 + nt] + time_step * total[1]
            out[1, t0 : t0 + nt] = row_b[1, t0 : t0 + nt] - time_step * total[0]

        if HALVES == 1:
            receive()
        else:
            pl.when(lax.rem(z, HALVES) == hf)(receive)

    compute(0)
    gather_rest(1, 1)
    compute(1)
    y_late(0)
    gather_rest(1, 2)
    gather_rest(1, 3)
    compute(2)
    y_late(1)
    z_send(0)
    compute(3)
    y_late(2)
    z_send(1)
    y_late(3)
    finish(0)
    z_send(2)
    finish(1)
    z_send(3)
    finish(2)
    finish(3)

    for hf in range(HALVES):
        for copy in g[hf]:
            copy.wait_send()
    for st in range(n_st):
        for copy in y_copies(st):
            copy.wait_send()
        z_each(st, lambda copy: copy.wait_send())


def on_device(
    lesser_hist, greater_hist, advanced_hist, current_row, adjacency, weight_table, step_index
):
    vmem, dma = pltpu.VMEM, pltpu.SemaphoreType.DMA
    n_st = len(STAGES)
    scratch = [
        vmem((2, NS, ROWS, COLS), f32),
        vmem((2, NS, COLS, ROWS), f32),
        vmem((NT, 2, NS, 256, COLS), f32),
        vmem((2, NT, 8, COLS), f32),
        vmem((8, 256), jnp.int32),
        vmem((HALVES, 8, NS, 2, RB, COLS), f32),
        vmem((HALVES, 2, NS, 2, 4, RB, COLS), bf16),
        vmem((HALVES, 2, NS, 2, 4, RB, COLS), bf16),
        vmem((NT, NS, 256, 256), bf16),
        vmem((NT, NS, 256, 256), bf16),
        vmem((HALVES, 4 * RB, 128), bf16),
        vmem((NT, 128, 256), bf16),
        dma((4,)), dma((NT,)),
        dma((HALVES, 13)), dma((HALVES, 13)),
        dma((n_st, 6)), dma((n_st, 6)),
        dma((n_st, NZ - 1)), dma((n_st, NZ - 1)),
    ]
    scratch += [vmem((NY, NZZ, 2, nt, 8, COLS), f32) for _, _, nt in STAGES]
    scratch += [vmem((2, NZZ // 2, 2, nt, 8, COLS), f32) for _, _, nt in STAGES]
    scratch += [vmem((2, NZZ, 2, nt, 8, COLS), f32) for _, _, nt in STAGES]
    scratch += [vmem((NZ - 1, 2, nt, 8, COLS), f32) for _, _, nt in STAGES]
    smem = pl.BlockSpec(memory_space=pltpu.SMEM)
    anywhere = pl.BlockSpec(memory_space=pl.ANY)
    return pl.pallas_call(
        kernel,
        out_shape=jax.ShapeDtypeStruct((2, NT, 8, COLS), f32),
        in_specs=[smem, smem] + [anywhere] * 5,
        out_specs=pl.BlockSpec(memory_space=vmem),
        scratch_shapes=scratch,
        compiler_params=pltpu.CompilerParams(
            collective_id=0, has_side_effects=True, vmem_limit_bytes=56 * 1024 * 1024
        ),
        name="row_step",
    )(weight_table, step_index, lesser_hist, greater_hist, advanced_hist, current_row, adjacency)


def solution(mesh):
    in_specs = (
        P(None, "hist", "ocol", "orow"),
        P(None, "hist", "orow", "ocol"),
        P(None, "hist", "ocol", None, "orow"),
        P(None, "ocol", "hist", "orow"),
        P("hist", None),
        P("hist"),
        P(),
    )
    out_specs = P(None, "ocol", "hist", "orow")
    return jax.shard_map(
        on_device, mesh=mesh, in_specs=in_specs, out_specs=out_specs, check_vma=False
    )
```

```python
import jax
import jax.numpy as jnp
from jax import lax
from jax.experimental import pallas as pl
from jax.experimental.pallas import tpu as pltpu
from jax.sharding import PartitionSpec as P

coupling_square = 0.25
hopping = 4.0
time_step = 0.01

NZ, NY = 8, 4
NS, NT = 4, 8
ROWS, COLS = 64, 128
HALVES = 2
STAGES = (("D", 0, 0, 2), ("A", 0, 2, 4), ("B", 0, 6, 2), ("B", 1, 0, 4), ("B", 1, 4, 4))
G = -1
PLAN = (0, 1, 2, G, G, G, 3, 4, 1, 0, 2, 1, 3, 2, 0, 4, 1, 3, 4, 1, 2, 1, 3, 4)
MESH = pl.DeviceIdType.MESH
f32, bf16 = jnp.float32, jnp.bfloat16


def split(x):
    hi = x.astype(bf16)
    return hi, (x - hi.astype(f32)).astype(bf16)


def upper(shape):
    return lax.broadcasted_iota(jnp.int32, shape, len(shape) - 2) % 8 < 4


def swapped(x):
    tiles = x.reshape(x.shape[0] // 8, 8, x.shape[1])
    return pltpu.roll(tiles, 4, 1).reshape(x.shape)


def kernel(
    table_h, step_h, lesser, greater, advanced, row, adjacency, out,
    table, step, les_b, gre_b, adv_b, row_b, adj_b, gath, lhs_hi, lhs_lo, rhs_hi, rhs_lo, hop_l, hop_r,
    in_sem, adv_sem, gs, gr, *bufs,
):
    h, r, c = (lax.axis_index(a) for a in ("hist", "orow", "ocol"))
    z, y = lax.div(h, NY), lax.rem(h, NY)
    x, k = lax.div(c, 2) * 2 + r, lax.rem(c, 2)

    def wrap(v, n):
        return lax.rem(v + n, n)

    def dev(dx=0, dy=0, dz=0, other=False):
        xx = wrap(x + dx, 4)
        kk = 1 - k if other else k
        hh = wrap(z + dz, NZ) * NY + wrap(y + dy, NY)
        return (hh, lax.rem(xx, 2), lax.div(xx, 2) * 2 + kk)

    def remote(src, dst, ss, rs, to):
        return pltpu.make_async_remote_copy(
            src_ref=src, dst_ref=dst, send_sem=ss, recv_sem=rs, device_id=to, device_id_type=MESH
        )

    inputs = [
        pltpu.make_async_copy(a, b, in_sem.at[i])
        for i, (a, b) in enumerate(
            ((table_h, table), (step_h, step), (lesser, les_b), (greater, gre_b), (row, row_b), (adjacency, adj_b))
        )
    ]
    for copy in inputs:
        copy.start()
    adv = [pltpu.make_async_copy(advanced.at[:, :, t], adv_b.at[t], adv_sem.at[t]) for t in range(NT)]
    for copy in adv:
        copy.start()

    barrier = pltpu.get_barrier_semaphore()
    friends = [dev(dx=1), dev(dx=-1), dev(other=True), dev(dy=1), dev(dy=-1), dev(dy=2)]
    friends += [dev(dz=d) for d in range(1, NZ)]
    for friend in friends:
        pl.semaphore_signal(barrier, inc=1, device_id=friend, device_id_type=MESH)

    for copy in inputs[:4]:
        copy.wait()
    above = upper((ROWS, COLS))
    for s in range(NS):
        used = h * NS + s <= step[0]
        scale = jnp.where(used, table[s], 0).astype(f32) * (coupling_square / 24.0)
        lr, li = les_b[0, s], les_b[1, s]
        gre, gim = gre_b[0, s], gre_b[1, s]
        sr = (lr * lr - li * li) * scale
        si = (2.0 * lr * li) * scale
        re = sr * gre - si * gim
        im = sr * gim + si * gre
        gath[0, 0, s] = jnp.where(above, re, swapped(im))
        gath[1, 0, s] = jnp.where(above, swapped(re), im)

    pl.semaphore_wait(barrier, len(friends))

    slot_of = {0: (0, False), 1: (0, True), 2: (-1, False), 3: (-1, True),
               4: (1, False), 5: (1, True), 6: (2, False), 7: (2, True)}
    lo_s, hi_s, all_s = pl.ds(0, 2), pl.ds(2, 2), pl.ds(0, 4)
    right, left, twin = dev(dx=1), dev(dx=-1), dev(other=True)
    pieces = (
        (0, 2, lo_s, right), (0, 4, hi_s, left), (0, 2, hi_s, right), (0, 4, lo_s, left), (0, 1, all_s, twin),
        (2, 6, lo_s, right), (4, 6, hi_s, left),
        (2, 3, lo_s, twin), (4, 5, hi_s, twin), (2, 3, hi_s, twin), (4, 5, lo_s, twin),
        (6, 7, lo_s, twin), (6, 7, hi_s, twin),
    )

    def piece(hf, n):
        a, b, ss, to = pieces[n]
        return remote(gath.at[hf, a, ss], gath.at[hf, b, ss], gs.at[hf, n], gr.at[hf, n], to)

    def to_lhs(hf, slot, s_range=range(NS)):
        dx, other = slot_of[slot]
        xx = wrap(x + dx, 4)
        kh = dx % 2
        block = lax.div(xx, 2) * 2 + (1 - k if other else k)
        for s in s_range:
            v = gath[hf, slot, s]
            turned = swapped(v)
            for cc, part_v in enumerate((v, jnp.where(above, -turned, turned))):
                hi, lo = split(part_v)
                lhs_hi[hf, s, cc, kh, block] = hi
                lhs_lo[hf, s, cc, kh, block] = lo

    def begin(hf, names):
        for n in names:
            piece(hf, n).start()

    def arrived(hf, names):
        for n in names:
            piece(hf, n).wait_recv()

    def to_rhs(first, count):
        def one(pair, carry):
            for t in range(2):
                for s in range(NS):
                    for cc in range(2):
                        for kh in range(2):
                            rows = pl.ds(pl.multiple_of(wrap(r + kh, 2) * 128, 128), 128)
                            hi, lo = split(adv_b[2 * pair + t, cc, s, rows, :])
                            at = cc * 256 + kh * 128
                            rhs_hi[pair, s, at : at + 128, t * 128 : (t + 1) * 128] = hi
                            rhs_lo[pair, s, at : at + 128, t * 128 : (t + 1) * 128] = lo
            return carry

        for t in range(2 * first, 2 * (first + count)):
            adv[t].wait()
        lax.fori_loop(first, first + count, one, 0)

    begin(0, (0, 1, 2, 3, 4))
    begin(1, (0, 1))

    inputs[4].wait()
    inputs[5].wait()
    adj = adj_b[...].astype(f32) * -hopping
    adj_t = jnp.concatenate([adj, adj, adj, adj, jnp.zeros((96, 256), f32)], axis=0).T
    adj_s = swapped(adj_t)
    top = upper((256, 128))
    lane = lax.broadcasted_iota(jnp.int32, (256, 128), 1)
    keep = top == (lane < 16)
    hop_l[0] = jnp.where(keep, jnp.where(top, adj_t, adj_s), 0.0).astype(bf16)
    hop_l[1] = jnp.where(keep, jnp.where(top, adj_s, adj_t), 0.0).astype(bf16)
    for pair in range(NT // 2):
        rows = []
        for cc in range(2):
            v = jnp.concatenate([row_b[cc, 2 * pair], row_b[cc, 2 * pair + 1]], axis=1)
            hi = v.astype(bf16).astype(f32)
            rows += [hi, v - hi]
        rows.append(jnp.zeros((96, 256), f32))
        hop_r[pair] = jnp.concatenate(rows, axis=0).astype(bf16)

    to_lhs(0, 0)
    to_rhs(0, 2)

    def gather_rest(hf, step_n):
        if step_n == 0:
            arrived(hf, (0, 1))
            begin(hf, (5, 6, 7, 8))
        elif step_n == 1:
            arrived(hf, (2, 3))
            begin(hf, (9, 10))
            to_lhs(hf, 2)
            to_lhs(hf, 4)
            arrived(hf, (4,))
            to_lhs(hf, 1)
        elif step_n == 2:
            arrived(hf, (5, 6))
            begin(hf, (11, 12))
            to_lhs(hf, 6)
            arrived(hf, (7, 8, 9, 10))
            to_lhs(hf, 3)
            to_lhs(hf, 5)
        else:
            arrived(hf, (11, 12))
            to_lhs(hf, 7)

    gather_rest(0, 0)
    begin(1, (2, 3, 4))
    to_lhs(1, 0)
    to_rhs(2, 2)
    gather_rest(0, 1)
    gather_rest(1, 0)
    gather_rest(0, 2)
    gather_rest(0, 3)

    def product(st, store):
        _, hf, t0, nt = STAGES[st]

        def one(i, carry):
            pair = t0 // 2 + i
            acc = jnp.dot(hop_l[hf], hop_r[pair], preferred_element_type=f32)
            for s in range(NS):
                def left_of(ref):
                    a = [ref[hf, s, cc, kh].reshape(256, 128) for cc in range(2) for kh in range(2)]
                    return jnp.concatenate(a, axis=1)

                a_hi, a_lo = left_of(lhs_hi), left_of(lhs_lo)
                b_hi, b_lo = rhs_hi[pair, s], rhs_lo[pair, s]
                for a, b in ((a_hi, b_hi), (a_hi, b_lo), (a_lo, b_hi)):
                    acc = acc + jnp.dot(a, b, preferred_element_type=f32)
            for t in range(2):
                store(acc[:, t * 128 : (t + 1) * 128].reshape(NZ, NY, 8, 128), 2 * i + t)
            return carry

        lax.fori_loop(0, nt // 2, one, 0)

    def finish(st, total):
        _, hf, t0, nt = STAGES[st]
        total = total.reshape(nt * 8, 128)
        turned = swapped(total) * time_step
        change = jnp.where(upper(total.shape), turned, -turned).reshape(nt, 8, 128)
        rows = slice(4 * hf, 4 * hf + 4)
        for cc in range(2):
            mine = row_b[cc, t0 : t0 + nt, rows] + change[:, 4 * cc : 4 * cc + 4]
            out[cc, t0 : t0 + nt, rows] = mine

    class Stage:
        def __init__(self, st, refs):
            self.st, self.refs, self.sems = st, refs[:-2], refs[-2:]
            self.table = self.copies()
            self.steps = self.program()

        def copy(self, n):
            src, dst, to = self.table[n]()
            return remote(src, dst, self.sems[0].at[n], self.sems[1].at[n], to)

        def start(self, *names):
            for n in names:
                self.copy(n).start()

        def got(self, *names):
            for n in names:
                self.copy(n).wait_recv()

        def next(self):
            self.steps.pop(0)()

        def sent(self):
            for n in range(len(self.table)):
                self.copy(n).wait_send()

    def last_z(p, slots):
        return [
            lambda d=d: (p.at[y, wrap(z + d, NZ)], slots.at[d - 1], dev(dz=d)) for d in range(1, NZ)
        ]

    def ascending(stage, first):
        p, slots = stage.refs[0], stage.refs[-1]
        for to in range(NZ):
            @pl.when(z != to)
            def _():
                d = wrap(to - z, NZ)
                ss, rs = (s.at[first + d - 1] for s in stage.sems)
                remote(p.at[y, to], slots.at[d - 1], ss, rs, (to * NY + y, r, c)).start()

    class B(Stage):
        def copies(self):
            p, one, two, slots = self.refs
            lo, hi = pl.ds(0, NZ // 2), pl.ds(NZ // 2, NZ // 2)
            up, down = dev(dy=1), dev(dy=-1)
            y1, y2, y3 = wrap(y + 1, NY), wrap(y + 2, NY), wrap(y - 1, NY)
            return [
                lambda: (p.at[y2, lo], one.at[0], up),
                lambda: (p.at[y2, hi], one.at[1], down),
                lambda: (p.at[y1, hi], two.at[0, hi], up),
                lambda: (p.at[y3, lo], two.at[1, lo], down),
                lambda: (p.at[y1, lo], two.at[0, lo], up),
                lambda: (p.at[y3, hi], two.at[1, hi], down),
            ] + last_z(p, slots)

        def program(self):
            p, one, two, slots = self.refs

            def first():
                def store(v, t):
                    for yy in range(NY):
                        p[yy, :, t] = v[:, yy]

                product(self.st, store)
                self.start(0, 1, 2, 3)

            def late():
                n = NZ // 2
                y1, y3 = wrap(y + 1, NY), wrap(y - 1, NY)
                self.got(0)
                p[y1, :n] = p[y1, :n] + one[0]
                self.start(4)
                self.got(1)
                p[y3, n:] = p[y3, n:] + one[1]
                self.start(5)

            def send():
                self.got(2, 3, 4, 5)
                p[y] = p[y] + two[0] + two[1]
                ascending(self, 6)

            def end():
                self.got(*range(6, 6 + NZ - 1))
                total = p[y, z]
                for d in range(NZ - 1):
                    total = total + slots[d]
                finish(self.st, total)

            return [first, late, send, end]

    class D(Stage):
        def copies(self):
            p, two, slots = self.refs
            return [
                lambda d=d: (p.at[wrap(y + d, NY)], two.at[d - 1], dev(dy=d)) for d in range(1, NY)
            ] + last_z(p, slots)

        def program(self):
            p, two, slots = self.refs

            def first():
                def store(v, t):
                    for yy in range(NY):
                        p[yy, :, t] = v[:, yy]

                product(self.st, store)
                self.start(*range(NY - 1))

            def send():
                self.got(*range(NY - 1))
                p[y] = p[y] + two[0] + two[1] + two[2]
                ascending(self, NY - 1)

            def end():
                self.got(*range(NY - 1, NY + NZ - 2))
                total = p[y, z]
                for d in range(NZ - 1):
                    total = total + slots[d]
                finish(self.st, total)

            return [first, send, end]

    class A(Stage):
        def copies(self):
            p, one, two, three, four, slots = self.refs
            lo, hi = pl.ds(0, NY // 2), pl.ds(NY // 2, NY // 2)
            up, down = dev(dz=1), dev(dz=-1)

            def at(d):
                return wrap(z + d, NZ)

            return [
                lambda: (p.at[at(4), lo], one.at[0], up),
                lambda: (p.at[at(4), hi], one.at[1], down),
                lambda: (p.at[at(3), hi], two.at[0, hi], up),
                lambda: (p.at[at(-3), lo], two.at[1, lo], down),
                lambda: (p.at[at(3), lo], two.at[0, lo], up),
                lambda: (p.at[at(-3), hi], two.at[1, hi], down),
                lambda: (p.at[at(2)], three.at[0], up),
                lambda: (p.at[at(-2)], three.at[1], down),
                lambda: (p.at[at(1)], four.at[0], up),
                lambda: (p.at[at(-1)], four.at[1], down),
            ] + [
                lambda d=d: (p.at[z, wrap(y + d, NY)], slots.at[d - 1], dev(dy=d)) for d in range(1, NY)
            ]

        def program(self):
            p, one, two, three, four, slots = self.refs
            n = NY // 2

            def at(d):
                return wrap(z + d, NZ)

            def first():
                def store(v, t):
                    p[:, :, t] = v

                product(self.st, store)
                self.start(0, 1, 2, 3)

            def second():
                self.got(0)
                p[at(3), :n] = p[at(3), :n] + one[0]
                self.start(4)
                self.got(1)
                p[at(-3), n:] = p[at(-3), n:] + one[1]
                self.start(5)

            def third():
                self.got(2, 4)
                p[at(2)] = p[at(2)] + two[0]
                self.start(6)
                self.got(3, 5)
                p[at(-2)] = p[at(-2)] + two[1]
                self.start(7)

            def fourth():
                self.got(6)
                p[at(1)] = p[at(1)] + three[0]
                self.start(8)
                self.got(7)
                p[at(-1)] = p[at(-1)] + three[1]
                self.start(9)

            def send():
                self.got(8, 9)
                p[z] = p[z] + four[0] + four[1]
                self.start(10, 11, 12)

            def end():
                self.got(10, 11, 12)
                finish(self.st, p[z, y] + slots[0] + slots[1] + slots[2])

            return [first, second, third, fourth, send, end]

    stages, used_refs = [], 0
    for st, (kind, _, _, _) in enumerate(STAGES):
        count = len(stage_scratch(STAGES[st]))
        stages.append({"A": A, "B": B, "D": D}[kind](st, bufs[used_refs : used_refs + count]))
        used_refs += count
    gather_step = 1
    for name in PLAN:
        if name == G:
            gather_rest(1, gather_step)
            gather_step += 1
        else:
            stages[name].next()

    for hf in range(HALVES):
        for n in range(len(pieces)):
            piece(hf, n).wait_send()
    for stage in stages:
        stage.sent()


def stage_scratch(stage):
    kind, _, _, nt = stage
    dma = pltpu.SemaphoreType.DMA

    def block(*lead):
        return pltpu.VMEM((*lead, nt, 8, COLS), f32)

    if kind == "A":
        ring = [block(2, NY // 2), block(2, NY), block(2, NY), block(2, NY)]
        return [block(NZ, NY), *ring, block(NY - 1), dma((13,)), dma((13,))]
    if kind == "B":
        return [block(NY, NZ), block(2, NZ // 2), block(2, NZ), block(NZ - 1), dma((13,)), dma((13,))]
    return [block(NY, NZ), block(NY - 1, NZ), block(NZ - 1), dma((10,)), dma((10,))]


def on_device(
    lesser_hist, greater_hist, advanced_hist, current_row, adjacency, weight_table, step_index
):
    vmem, dma, smem = pltpu.VMEM, pltpu.SemaphoreType.DMA, pltpu.SMEM
    lhs = vmem((HALVES, NS, 2, 2, 4, ROWS, COLS), bf16)
    rhs = vmem((NT // 2, NS, 512, 256), bf16)
    scratch = [
        smem((NS,), jnp.int32),
        smem((1,), jnp.int32),
        vmem((2, NS, ROWS, COLS), f32),
        vmem((2, NS, ROWS, COLS), f32),
        vmem((NT, 2, NS, 256, COLS), f32),
        vmem((2, NT, 8, COLS), f32),
        vmem((8, 256), jnp.int32),
        vmem((HALVES, 8, NS, ROWS, COLS), f32),
        lhs, lhs, rhs, rhs,
        vmem((HALVES, 256, 128), bf16),
        vmem((NT // 2, 128, 256), bf16),
        dma((6,)), dma((NT,)), dma((HALVES, 13)), dma((HALVES, 13)),
    ]
    for stage in STAGES:
        scratch += stage_scratch(stage)
    return pl.pallas_call(
        kernel,
        out_shape=jax.ShapeDtypeStruct((2, NT, 8, COLS), f32),
        in_specs=[pl.BlockSpec(memory_space=pl.ANY)] * 7,
        out_specs=pl.BlockSpec(memory_space=vmem),
        scratch_shapes=scratch,
        compiler_params=pltpu.CompilerParams(
            collective_id=0, has_side_effects=True, vmem_limit_bytes=56 * 1024 * 1024
        ),
        name="row_step",
    )(
        weight_table, step_index, lesser_hist, jnp.swapaxes(greater_hist, 2, 3), advanced_hist,
        current_row, adjacency,
    )


def solution(mesh):
    in_specs = (
        P(None, "hist", "ocol", "orow"),
        P(None, "hist", "orow", "ocol"),
        P(None, "hist", "ocol", None, "orow"),
        P(None, "ocol", "hist", "orow"),
        P("hist", None),
        P("hist"),
        P(),
    )
    out_specs = P(None, "ocol", "hist", "orow")
    return jax.shard_map(
        on_device, mesh=mesh, in_specs=in_specs, out_specs=out_specs, check_vma=False
    )
```

```python
import jax
import jax.numpy as jnp
from jax import lax
from jax.experimental import pallas as pl
from jax.experimental.pallas import tpu as pltpu
from jax.sharding import PartitionSpec as P

coupling_square = 0.25
hopping = 4.0
time_step = 0.01

NZ, NY = 8, 4
NS, NT = 4, 8
ROWS, COLS = 64, 128
HALVES = 2
STAGES = (("D", 0, 0, 2), ("A", 0, 2, 4), ("B", 0, 6, 2), ("B", 1, 0, 4), ("B", 1, 4, 4))
G = -1
PLAN = (0, 1, 2, G, G, G, 3, 4, 1, 0, 2, 1, 3, 2, 0, 4, 1, 3, 4, 1, 2, 1, 3, 4)
MESH = pl.DeviceIdType.MESH
f32, bf16 = jnp.float32, jnp.bfloat16


def split(x):
    hi = x.astype(bf16)
    return hi, (x - hi.astype(f32)).astype(bf16)


def upper(shape):
    return lax.broadcasted_iota(jnp.int32, shape, len(shape) - 2) % 8 < 4


def swapped(x):
    tiles = x.reshape(x.shape[0] // 8, 8, x.shape[1])
    return pltpu.roll(tiles, 4, 1).reshape(x.shape)


def kernel(
    table_h, step_h, lesser, greater, advanced, row, adjacency, out,
    table, step, les_b, gre_b, adv_b, row_b, adj_b, gath, lhs_hi, lhs_lo, rhs_hi, rhs_lo, hop_l, hop_r,
    in_sem, adv_sem, gs, gr, *bufs,
):
    h, r, c = (lax.axis_index(a) for a in ("hist", "orow", "ocol"))
    z, y = lax.div(h, NY), lax.rem(h, NY)
    x, k = lax.div(c, 2) * 2 + r, lax.rem(c, 2)

    def wrap(v, n):
        return lax.rem(v + n, n)

    def dev(dx=0, dy=0, dz=0, other=False):
        xx = wrap(x + dx, 4)
        kk = 1 - k if other else k
        hh = wrap(z + dz, NZ) * NY + wrap(y + dy, NY)
        return (hh, lax.rem(xx, 2), lax.div(xx, 2) * 2 + kk)

    def remote(src, dst, ss, rs, to):
        return pltpu.make_async_remote_copy(
            src_ref=src, dst_ref=dst, send_sem=ss, recv_sem=rs, device_id=to, device_id_type=MESH
        )

    inputs = [
        pltpu.make_async_copy(a, b, in_sem.at[i])
        for i, (a, b) in enumerate(
            ((table_h, table), (step_h, step), (lesser, les_b), (greater, gre_b), (row, row_b), (adjacency, adj_b))
        )
    ]
    for copy in inputs:
        copy.start()
    adv = [pltpu.make_async_copy(advanced.at[:, :, t], adv_b.at[t], adv_sem.at[t]) for t in range(NT)]
    for copy in adv:
        copy.start()

    barrier = pltpu.get_barrier_semaphore()
    friends = [dev(dx=1), dev(dx=-1), dev(other=True), dev(dy=1), dev(dy=-1), dev(dy=2)]
    friends += [dev(dz=d) for d in range(1, NZ)]
    for friend in friends:
        pl.semaphore_signal(barrier, inc=1, device_id=friend, device_id_type=MESH)

    for copy in inputs[:4]:
        copy.wait()
    above = upper((ROWS, COLS))
    for s in range(NS):
        used = h * NS + s <= step[0]
        scale = jnp.where(used, table[s], 0).astype(f32) * (coupling_square / 24.0)
        lr, li = les_b[0, s], les_b[1, s]
        gre, gim = gre_b[0, s], gre_b[1, s]
        sr = (lr * lr - li * li) * scale
        si = (2.0 * lr * li) * scale
        re = sr * gre - si * gim
        im = sr * gim + si * gre
        gath[0, 0, s] = jnp.where(above, re, swapped(im))
        gath[1, 0, s] = jnp.where(above, swapped(re), im)

    pl.semaphore_wait(barrier, len(friends))

    slot_of = {0: (0, False), 1: (0, True), 2: (-1, False), 3: (-1, True),
               4: (1, False), 5: (1, True), 6: (2, False), 7: (2, True)}
    lo_s, hi_s, all_s = pl.ds(0, 2), pl.ds(2, 2), pl.ds(0, 4)
    right, left, twin = dev(dx=1), dev(dx=-1), dev(other=True)
    pieces = (
        (0, 2, lo_s, right), (0, 4, hi_s, left), (0, 2, hi_s, right), (0, 4, lo_s, left), (0, 1, all_s, twin),
        (2, 6, lo_s, right), (4, 6, hi_s, left),
        (2, 3, lo_s, twin), (4, 5, hi_s, twin), (2, 3, hi_s, twin), (4, 5, lo_s, twin),
        (6, 7, lo_s, twin), (6, 7, hi_s, twin),
    )

    def piece(hf, n):
        a, b, ss, to = pieces[n]
        return remote(gath.at[hf, a, ss], gath.at[hf, b, ss], gs.at[hf, n], gr.at[hf, n], to)

    def to_lhs(hf, slot, s_range=range(NS)):
        dx, other = slot_of[slot]
        xx = wrap(x + dx, 4)
        kh = dx % 2
        block = lax.div(xx, 2) * 2 + (1 - k if other else k)
        for s in s_range:
            v = gath[hf, slot, s]
            turned = swapped(v)
            for cc, part_v in enumerate((v, jnp.where(above, -turned, turned))):
                hi, lo = split(part_v)
                lhs_hi[hf, s, cc, kh, block] = hi
                lhs_lo[hf, s, cc, kh, block] = lo

    def begin(hf, names):
        for n in names:
            piece(hf, n).start()

    def arrived(hf, names):
        for n in names:
            piece(hf, n).wait_recv()

    def to_rhs(first, count):
        def one(pair, carry):
            for t in range(2):
                for s in range(NS):
                    for cc in range(2):
                        for kh in range(2):
                            rows = pl.ds(pl.multiple_of(wrap(r + kh, 2) * 128, 128), 128)
                            hi, lo = split(adv_b[2 * pair + t, cc, s, rows, :])
                            at = cc * 256 + kh * 128
                            rhs_hi[pair, s, at : at + 128, t * 128 : (t + 1) * 128] = hi
                            rhs_lo[pair, s, at : at + 128, t * 128 : (t + 1) * 128] = lo
            return carry

        for t in range(2 * first, 2 * (first + count)):
            adv[t].wait()
        lax.fori_loop(first, first + count, one, 0)

    begin(0, (0, 1, 2, 3, 4))
    begin(1, (0, 1))

    inputs[4].wait()
    inputs[5].wait()
    adj = adj_b[...].astype(f32) * -hopping
    adj_t = jnp.concatenate([adj, adj, adj, adj, jnp.zeros((96, 256), f32)], axis=0).T
    adj_s = swapped(adj_t)
    top = upper((256, 128))
    lane = lax.broadcasted_iota(jnp.int32, (256, 128), 1)
    keep = top == (lane < 16)
    hop_l[0] = jnp.where(keep, jnp.where(top, adj_t, adj_s), 0.0).astype(bf16)
    hop_l[1] = jnp.where(keep, jnp.where(top, adj_s, adj_t), 0.0).astype(bf16)
    for pair in range(NT // 2):
        rows = []
        for cc in range(2):
            v = jnp.concatenate([row_b[cc, 2 * pair], row_b[cc, 2 * pair + 1]], axis=1)
            hi = v.astype(bf16).astype(f32)
            rows += [hi, v - hi]
        rows.append(jnp.zeros((96, 256), f32))
        hop_r[pair] = jnp.concatenate(rows, axis=0).astype(bf16)

    to_lhs(0, 0)
    to_rhs(0, 2)

    def gather_rest(hf, step_n):
        if step_n == 0:
            arrived(hf, (0, 1))
            begin(hf, (5, 6, 7, 8))
        elif step_n == 1:
            arrived(hf, (2, 3))
            begin(hf, (9, 10))
            to_lhs(hf, 2)
            to_lhs(hf, 4)
            arrived(hf, (4,))
            to_lhs(hf, 1)
        elif step_n == 2:
            arrived(hf, (5, 6))
            begin(hf, (11, 12))
            to_lhs(hf, 6)
            arrived(hf, (7, 8, 9, 10))
            to_lhs(hf, 3)
            to_lhs(hf, 5)
        else:
            arrived(hf, (11, 12))
            to_lhs(hf, 7)

    gather_rest(0, 0)
    begin(1, (2, 3, 4))
    to_lhs(1, 0)
    to_rhs(2, 2)
    gather_rest(0, 1)
    gather_rest(1, 0)
    gather_rest(0, 2)
    gather_rest(0, 3)

    def product(st, store):
        _, hf, t0, nt = STAGES[st]

        def one(i, carry):
            pair = t0 // 2 + i
            acc = jnp.dot(hop_l[hf], hop_r[pair], preferred_element_type=f32)
            for s in range(NS):
                def left_of(ref):
                    a = [ref[hf, s, cc, kh].reshape(256, 128) for cc in range(2) for kh in range(2)]
                    return jnp.concatenate(a, axis=1)

                a_hi, a_lo = left_of(lhs_hi), left_of(lhs_lo)
                b_hi, b_lo = rhs_hi[pair, s], rhs_lo[pair, s]
                for a, b in ((a_hi, b_hi), (a_hi, b_lo), (a_lo, b_hi)):
                    acc = acc + jnp.dot(a, b, preferred_element_type=f32)
            for t in range(2):
                store(acc[:, t * 128 : (t + 1) * 128].reshape(NZ, NY, 8, 128), 2 * i + t)
            return carry

        lax.fori_loop(0, nt // 2, one, 0)

    def finish(st, total):
        _, hf, t0, nt = STAGES[st]
        total = total.reshape(nt * 8, 128)
        turned = swapped(total) * time_step
        change = jnp.where(upper(total.shape), turned, -turned).reshape(nt, 8, 128)
        rows = slice(4 * hf, 4 * hf + 4)
        for cc in range(2):
            mine = row_b[cc, t0 : t0 + nt, rows] + change[:, 4 * cc : 4 * cc + 4]
            out[cc, t0 : t0 + nt, rows] = mine

    class Stage:
        def __init__(self, st, refs):
            self.st, self.refs, self.sems = st, refs[:-2], refs[-2:]
            self.table = self.copies()
            self.steps = self.program()

        def copy(self, n):
            src, dst, to = self.table[n]()
            return remote(src, dst, self.sems[0].at[n], self.sems[1].at[n], to)

        def start(self, *names):
            for n in names:
                self.copy(n).start()

        def got(self, *names):
            for n in names:
                self.copy(n).wait_recv()

        def next(self):
            self.steps.pop(0)()

        def sent(self):
            for n in range(len(self.table)):
                self.copy(n).wait_send()

    def last_z(p, slots):
        return [
            lambda d=d: (p.at[y, wrap(z + d, NZ)], slots.at[d - 1], dev(dz=d)) for d in range(1, NZ)
        ]

    def ascending(stage, first, destinations=range(NZ)):
        p, slots = stage.refs[0], stage.refs[-1]
        for to in destinations:
            @pl.when(z != to)
            def _():
                d = wrap(to - z, NZ)
                ss, rs = (s.at[first + d - 1] for s in stage.sems)
                remote(p.at[y, to], slots.at[d - 1], ss, rs, (to * NY + y, r, c)).start()

    class B(Stage):
        def copies(self):
            p, one, two, slots = self.refs
            lo, hi = pl.ds(0, NZ // 2), pl.ds(NZ // 2, NZ // 2)
            up, down = dev(dy=1), dev(dy=-1)
            y1, y2, y3 = wrap(y + 1, NY), wrap(y + 2, NY), wrap(y - 1, NY)
            return [
                lambda: (p.at[y2, lo], one.at[0], up),
                lambda: (p.at[y2, hi], one.at[1], down),
                lambda: (p.at[y1, hi], two.at[0, hi], up),
                lambda: (p.at[y3, lo], two.at[1, lo], down),
                lambda: (p.at[y1, lo], two.at[0, lo], up),
                lambda: (p.at[y3, hi], two.at[1, hi], down),
            ] + last_z(p, slots)

        def program(self):
            p, one, two, slots = self.refs

            def first():
                def store(v, t):
                    for yy in range(NY):
                        p[yy, :, t] = v[:, yy]

                product(self.st, store)
                self.start(0, 1, 2, 3)

            def late():
                n = NZ // 2
                y1, y3 = wrap(y + 1, NY), wrap(y - 1, NY)
                self.got(0)
                p[y1, :n] = p[y1, :n] + one[0]
                self.start(4)
                self.got(1)
                p[y3, n:] = p[y3, n:] + one[1]
                self.start(5)

            def send():
                n = NZ // 2
                self.got(3, 4)
                p[y, :n] = p[y, :n] + two[0, :n] + two[1, :n]
                ascending(self, 6, range(n))
                self.got(2, 5)
                p[y, n:] = p[y, n:] + two[0, n:] + two[1, n:]
                ascending(self, 6, range(n, NZ))

            def end():
                self.got(*range(6, 6 + NZ - 1))
                total = p[y, z]
                for d in range(NZ - 1):
                    total = total + slots[d]
                finish(self.st, total)

            return [first, late, send, end]

    class D(Stage):
        def copies(self):
            p, two, slots = self.refs
            return [
                lambda d=d: (p.at[wrap(y + d, NY)], two.at[d - 1], dev(dy=d)) for d in range(1, NY)
            ] + last_z(p, slots)

        def program(self):
            p, two, slots = self.refs

            def first():
                def store(v, t):
                    for yy in range(NY):
                        p[yy, :, t] = v[:, yy]

                product(self.st, store)
                self.start(*range(NY - 1))

            def send():
                self.got(*range(NY - 1))
                p[y] = p[y] + two[0] + two[1] + two[2]
                ascending(self, NY - 1)

            def end():
                self.got(*range(NY - 1, NY + NZ - 2))
                total = p[y, z]
                for d in range(NZ - 1):
                    total = total + slots[d]
                finish(self.st, total)

            return [first, send, end]

    class A(Stage):
        def copies(self):
            p, one, two, three, four, slots = self.refs
            lo, hi = pl.ds(0, NY // 2), pl.ds(NY // 2, NY // 2)
            up, down = dev(dz=1), dev(dz=-1)

            def at(d):
                return wrap(z + d, NZ)

            return [
                lambda: (p.at[at(4), lo], one.at[0], up),
                lambda: (p.at[at(4), hi], one.at[1], down),
                lambda: (p.at[at(3), hi], two.at[0, hi], up),
                lambda: (p.at[at(-3), lo], two.at[1, lo], down),
                lambda: (p.at[at(3), lo], two.at[0, lo], up),
                lambda: (p.at[at(-3), hi], two.at[1, hi], down),
                lambda: (p.at[at(2)], three.at[0], up),
                lambda: (p.at[at(-2)], three.at[1], down),
                lambda: (p.at[at(1)], four.at[0], up),
                lambda: (p.at[at(-1)], four.at[1], down),
            ] + [
                lambda d=d: (p.at[z, wrap(y + d, NY)], slots.at[d - 1], dev(dy=d)) for d in range(1, NY)
            ]

        def program(self):
            p, one, two, three, four, slots = self.refs
            n = NY // 2

            def at(d):
                return wrap(z + d, NZ)

            def first():
                def store(v, t):
                    p[:, :, t] = v

                product(self.st, store)
                self.start(0, 1, 2, 3)

            def second():
                self.got(0)
                p[at(3), :n] = p[at(3), :n] + one[0]
                self.start(4)
                self.got(1)
                p[at(-3), n:] = p[at(-3), n:] + one[1]
                self.start(5)

            def third():
                self.got(2, 4)
                p[at(2)] = p[at(2)] + two[0]
                self.start(6)
                self.got(3, 5)
                p[at(-2)] = p[at(-2)] + two[1]
                self.start(7)

            def fourth():
                self.got(6)
                p[at(1)] = p[at(1)] + three[0]
                self.start(8)
                self.got(7)
                p[at(-1)] = p[at(-1)] + three[1]
                self.start(9)

            def send():
                self.got(8, 9)
                p[z] = p[z] + four[0] + four[1]
                self.start(10, 11, 12)

            def end():
                self.got(10, 11, 12)
                finish(self.st, p[z, y] + slots[0] + slots[1] + slots[2])

            return [first, second, third, fourth, send, end]

    stages, used_refs = [], 0
    for st, (kind, _, _, _) in enumerate(STAGES):
        count = len(stage_scratch(STAGES[st]))
        stages.append({"A": A, "B": B, "D": D}[kind](st, bufs[used_refs : used_refs + count]))
        used_refs += count
    gather_step = 1
    for name in PLAN:
        if name == G:
            gather_rest(1, gather_step)
            gather_step += 1
        else:
            stages[name].next()

    for hf in range(HALVES):
        for n in range(len(pieces)):
            piece(hf, n).wait_send()
    for stage in stages:
        stage.sent()


def stage_scratch(stage):
    kind, _, _, nt = stage
    dma = pltpu.SemaphoreType.DMA

    def block(*lead):
        return pltpu.VMEM((*lead, nt, 8, COLS), f32)

    if kind == "A":
        ring = [block(2, NY // 2), block(2, NY), block(2, NY), block(2, NY)]
        return [block(NZ, NY), *ring, block(NY - 1), dma((13,)), dma((13,))]
    if kind == "B":
        return [block(NY, NZ), block(2, NZ // 2), block(2, NZ), block(NZ - 1), dma((13,)), dma((13,))]
    return [block(NY, NZ), block(NY - 1, NZ), block(NZ - 1), dma((10,)), dma((10,))]


def on_device(
    lesser_hist, greater_hist, advanced_hist, current_row, adjacency, weight_table, step_index
):
    vmem, dma, smem = pltpu.VMEM, pltpu.SemaphoreType.DMA, pltpu.SMEM
    lhs = vmem((HALVES, NS, 2, 2, 4, ROWS, COLS), bf16)
    rhs = vmem((NT // 2, NS, 512, 256), bf16)
    scratch = [
        smem((NS,), jnp.int32),
        smem((1,), jnp.int32),
        vmem((2, NS, ROWS, COLS), f32),
        vmem((2, NS, ROWS, COLS), f32),
        vmem((NT, 2, NS, 256, COLS), f32),
        vmem((2, NT, 8, COLS), f32),
        vmem((8, 256), jnp.int32),
        vmem((HALVES, 8, NS, ROWS, COLS), f32),
        lhs, lhs, rhs, rhs,
        vmem((HALVES, 256, 128), bf16),
        vmem((NT // 2, 128, 256), bf16),
        dma((6,)), dma((NT,)), dma((HALVES, 13)), dma((HALVES, 13)),
    ]
    for stage in STAGES:
        scratch += stage_scratch(stage)
    return pl.pallas_call(
        kernel,
        out_shape=jax.ShapeDtypeStruct((2, NT, 8, COLS), f32),
        in_specs=[pl.BlockSpec(memory_space=pl.ANY)] * 7,
        out_specs=pl.BlockSpec(memory_space=vmem),
        scratch_shapes=scratch,
        compiler_params=pltpu.CompilerParams(
            collective_id=0, has_side_effects=True, vmem_limit_bytes=56 * 1024 * 1024
        ),
        name="row_step",
    )(
        weight_table, step_index, lesser_hist, jnp.swapaxes(greater_hist, 2, 3), advanced_hist,
        current_row, adjacency,
    )


def solution(mesh):
    in_specs = (
        P(None, "hist", "ocol", "orow"),
        P(None, "hist", "orow", "ocol"),
        P(None, "hist", "ocol", None, "orow"),
        P(None, "ocol", "hist", "orow"),
        P("hist", None),
        P("hist"),
        P(),
    )
    out_specs = P(None, "ocol", "hist", "orow")
    return jax.shard_map(
        on_device, mesh=mesh, in_specs=in_specs, out_specs=out_specs, check_vma=False
    )
```

```python
import jax
import jax.numpy as jnp
from jax import lax
from jax.experimental import pallas as pl
from jax.experimental.pallas import tpu as pltpu
from jax.sharding import PartitionSpec as P

coupling_square = 0.25
hopping = 4.0
time_step = 0.01

NZ, NY = 8, 4
NS, NT = 4, 8
ROWS, COLS = 64, 128
HALVES = 2
STAGES = (("D", 0, 0, 2), ("A", 0, 2, 4), ("B", 0, 6, 2), ("B", 1, 0, 4), ("B", 1, 4, 4))
G = -1
PLAN = (0, 1, 2, G, G, G, 3, 4, 1, 0, 2, 1, 3, 2, 0, 4, 1, 3, 4, 1, 2, 1, 3, 4)
MESH = pl.DeviceIdType.MESH
f32, bf16 = jnp.float32, jnp.bfloat16


def split(x):
    hi = x.astype(bf16)
    return hi, (x - hi.astype(f32)).astype(bf16)


def upper(shape):
    return lax.broadcasted_iota(jnp.int32, shape, len(shape) - 2) % 8 < 4


def swapped(x):
    tiles = x.reshape(x.shape[0] // 8, 8, x.shape[1])
    return pltpu.roll(tiles, 4, 1).reshape(x.shape)


def kernel(
    table_h, step_h, lesser, greater, advanced, row, adjacency, out,
    table, step, les_b, gre_b, adv_b, row_b, adj_b, gath, lhs_hi, lhs_lo, rhs_hi, rhs_lo, hop_l, hop_r,
    in_sem, adv_sem, gs, gr, *bufs,
):
    h, r, c = (lax.axis_index(a) for a in ("hist", "orow", "ocol"))
    z, y = lax.div(h, NY), lax.rem(h, NY)
    x, k = lax.div(c, 2) * 2 + r, lax.rem(c, 2)

    def wrap(v, n):
        return lax.rem(v + n, n)

    def dev(dx=0, dy=0, dz=0, other=False):
        xx = wrap(x + dx, 4)
        kk = 1 - k if other else k
        hh = wrap(z + dz, NZ) * NY + wrap(y + dy, NY)
        return (hh, lax.rem(xx, 2), lax.div(xx, 2) * 2 + kk)

    def remote(src, dst, ss, rs, to):
        return pltpu.make_async_remote_copy(
            src_ref=src, dst_ref=dst, send_sem=ss, recv_sem=rs, device_id=to, device_id_type=MESH
        )

    inputs = [
        pltpu.make_async_copy(a, b, in_sem.at[i])
        for i, (a, b) in enumerate(
            ((table_h, table), (step_h, step), (lesser, les_b), (greater, gre_b), (row, row_b), (adjacency, adj_b))
        )
    ]
    for copy in inputs:
        copy.start()
    adv = [pltpu.make_async_copy(advanced.at[:, :, t], adv_b.at[t], adv_sem.at[t]) for t in range(NT)]
    for copy in adv:
        copy.start()

    barrier = pltpu.get_barrier_semaphore()
    friends = [dev(dx=1), dev(dx=-1), dev(other=True), dev(dy=1), dev(dy=-1), dev(dy=2)]
    friends += [dev(dz=d) for d in range(1, NZ)]
    for friend in friends:
        pl.semaphore_signal(barrier, inc=1, device_id=friend, device_id_type=MESH)

    for copy in inputs[:4]:
        copy.wait()
    above = upper((ROWS, COLS))
    for s in range(NS):
        used = h * NS + s <= step[0]
        scale = jnp.where(used, table[s], 0).astype(f32) * (coupling_square / 24.0)
        lr, li = les_b[0, s], les_b[1, s]
        gre, gim = gre_b[0, s], gre_b[1, s]
        sr = (lr * lr - li * li) * scale
        si = (2.0 * lr * li) * scale
        re = sr * gre - si * gim
        im = sr * gim + si * gre
        gath[0, 0, s] = jnp.where(above, re, swapped(im))
        gath[1, 0, s] = jnp.where(above, swapped(re), im)

    pl.semaphore_wait(barrier, len(friends))

    slot_of = {0: (0, False), 1: (0, True), 2: (-1, False), 3: (-1, True),
               4: (1, False), 5: (1, True), 6: (2, False), 7: (2, True)}
    lo_s, hi_s, all_s = pl.ds(0, 2), pl.ds(2, 2), pl.ds(0, 4)
    right, left, twin = dev(dx=1), dev(dx=-1), dev(other=True)
    pieces = (
        (0, 2, lo_s, right), (0, 4, hi_s, left), (0, 2, hi_s, right), (0, 4, lo_s, left), (0, 1, all_s, twin),
        (2, 6, lo_s, right), (4, 6, hi_s, left),
        (2, 3, lo_s, twin), (4, 5, hi_s, twin), (2, 3, hi_s, twin), (4, 5, lo_s, twin),
        (6, 7, lo_s, twin), (6, 7, hi_s, twin),
    )

    def piece(hf, n):
        a, b, ss, to = pieces[n]
        return remote(gath.at[hf, a, ss], gath.at[hf, b, ss], gs.at[hf, n], gr.at[hf, n], to)

    def to_lhs(hf, slot, s_range=range(NS)):
        dx, other = slot_of[slot]
        xx = wrap(x + dx, 4)
        kh = dx % 2
        block = lax.div(xx, 2) * 2 + (1 - k if other else k)
        for s in s_range:
            v = gath[hf, slot, s]
            turned = swapped(v)
            for cc, part_v in enumerate((v, jnp.where(above, -turned, turned))):
                hi, lo = split(part_v)
                lhs_hi[hf, s, cc, kh, block] = hi
                lhs_lo[hf, s, cc, kh, block] = lo

    def begin(hf, names):
        for n in names:
            piece(hf, n).start()

    def arrived(hf, names):
        for n in names:
            piece(hf, n).wait_recv()

    def to_rhs(first, count):
        def one(pair, carry):
            for t in range(2):
                for s in range(NS):
                    for cc in range(2):
                        for kh in range(2):
                            rows = pl.ds(pl.multiple_of(wrap(r + kh, 2) * 128, 128), 128)
                            hi, lo = split(adv_b[2 * pair + t, cc, s, rows, :])
                            at = cc * 256 + kh * 128
                            rhs_hi[pair, s, at : at + 128, t * 128 : (t + 1) * 128] = hi
                            rhs_lo[pair, s, at : at + 128, t * 128 : (t + 1) * 128] = lo
            return carry

        for t in range(2 * first, 2 * (first + count)):
            adv[t].wait()
        lax.fori_loop(first, first + count, one, 0)

    begin(0, (0, 1, 2, 3, 4))
    begin(1, (0, 1))

    inputs[4].wait()
    inputs[5].wait()
    adj = adj_b[...].astype(f32) * -hopping
    adj_t = jnp.concatenate([adj, adj, adj, adj, jnp.zeros((96, 256), f32)], axis=0).T
    adj_s = swapped(adj_t)
    top = upper((256, 128))
    lane = lax.broadcasted_iota(jnp.int32, (256, 128), 1)
    keep = top == (lane < 16)
    hop_l[0] = jnp.where(keep, jnp.where(top, adj_t, adj_s), 0.0).astype(bf16)
    hop_l[1] = jnp.where(keep, jnp.where(top, adj_s, adj_t), 0.0).astype(bf16)
    for pair in range(NT // 2):
        rows = []
        for cc in range(2):
            v = jnp.concatenate([row_b[cc, 2 * pair], row_b[cc, 2 * pair + 1]], axis=1)
            hi = v.astype(bf16).astype(f32)
            rows += [hi, v - hi]
        rows.append(jnp.zeros((96, 256), f32))
        hop_r[pair] = jnp.concatenate(rows, axis=0).astype(bf16)

    to_lhs(0, 0)
    to_rhs(0, 2)

    def gather_rest(hf, step_n):
        if step_n == 0:
            arrived(hf, (0, 1))
            begin(hf, (5, 6, 7, 8))
        elif step_n == 1:
            arrived(hf, (2, 3))
            begin(hf, (9, 10))
            to_lhs(hf, 2)
            to_lhs(hf, 4)
            arrived(hf, (4,))
            to_lhs(hf, 1)
        elif step_n == 2:
            arrived(hf, (5, 6))
            begin(hf, (11, 12))
            to_lhs(hf, 6)
            arrived(hf, (7, 8, 9, 10))
            to_lhs(hf, 3)
            to_lhs(hf, 5)
        else:
            arrived(hf, (11, 12))
            to_lhs(hf, 7)

    gather_rest(0, 0)
    begin(1, (2, 3, 4))
    to_lhs(1, 0)
    to_rhs(2, 2)
    gather_rest(0, 1)
    gather_rest(1, 0)
    gather_rest(0, 2)
    gather_rest(0, 3)

    def product(st, store):
        _, hf, t0, nt = STAGES[st]

        def one(i, carry):
            pair = t0 // 2 + i
            acc = jnp.dot(hop_l[hf], hop_r[pair], preferred_element_type=f32)
            for s in range(NS):
                def left_of(ref):
                    a = [ref[hf, s, cc, kh].reshape(256, 128) for cc in range(2) for kh in range(2)]
                    return jnp.concatenate(a, axis=1)

                a_hi, a_lo = left_of(lhs_hi), left_of(lhs_lo)
                b_hi, b_lo = rhs_hi[pair, s], rhs_lo[pair, s]
                for a, b in ((a_hi, b_hi), (a_hi, b_lo), (a_lo, b_hi)):
                    acc = acc + jnp.dot(a, b, preferred_element_type=f32)
            for t in range(2):
                store(acc[:, t * 128 : (t + 1) * 128].reshape(NZ, NY, 8, 128), 2 * i + t)
            return carry

        lax.fori_loop(0, nt // 2, one, 0)

    def finish(st, total):
        _, hf, t0, nt = STAGES[st]
        total = total.reshape(nt * 8, 128)
        turned = swapped(total) * time_step
        change = jnp.where(upper(total.shape), turned, -turned).reshape(nt, 8, 128)
        rows = slice(4 * hf, 4 * hf + 4)
        for cc in range(2):
            mine = row_b[cc, t0 : t0 + nt, rows] + change[:, 4 * cc : 4 * cc + 4]
            out[cc, t0 : t0 + nt, rows] = mine

    class Stage:
        def __init__(self, st, refs):
            self.st, self.refs, self.sems = st, refs[:-2], refs[-2:]
            self.table = self.copies()
            self.steps = self.program()

        def copy(self, n):
            src, dst, to = self.table[n]()
            return remote(src, dst, self.sems[0].at[n], self.sems[1].at[n], to)

        def start(self, *names):
            for n in names:
                self.copy(n).start()

        def got(self, *names):
            for n in names:
                self.copy(n).wait_recv()

        def next(self):
            self.steps.pop(0)()

        def sent(self):
            for n in range(len(self.table)):
                self.copy(n).wait_send()

    def last_z(p, slots):
        return [
            lambda d=d: (p.at[y, wrap(z + d, NZ)], slots.at[d - 1], dev(dz=d)) for d in range(1, NZ)
        ]

    def ascending(stage, first):
        p, slots = stage.refs[0], stage.refs[-1]
        for to in range(NZ):
            @pl.when(z != to)
            def _():
                d = wrap(to - z, NZ)
                ss, rs = (s.at[first + d - 1] for s in stage.sems)
                remote(p.at[y, to], slots.at[d - 1], ss, rs, (to * NY + y, r, c)).start()

    class B(Stage):
        def copies(self):
            p, one, two, slots = self.refs
            lo, hi = pl.ds(0, NZ // 2), pl.ds(NZ // 2, NZ // 2)
            up, down = dev(dy=1), dev(dy=-1)
            y1, y2, y3 = wrap(y + 1, NY), wrap(y + 2, NY), wrap(y - 1, NY)
            return [
                lambda: (p.at[y2, lo], one.at[0], up),
                lambda: (p.at[y2, hi], one.at[1], down),
                lambda: (p.at[y1, hi], two.at[0, hi], up),
                lambda: (p.at[y3, lo], two.at[1, lo], down),
                lambda: (p.at[y1, lo], two.at[0, lo], up),
                lambda: (p.at[y3, hi], two.at[1, hi], down),
            ] + last_z(p, slots)

        def program(self):
            p, one, two, slots = self.refs

            def first():
                def store(v, t):
                    for yy in range(NY):
                        p[yy, :, t] = v[:, yy]

                product(self.st, store)
                self.start(0, 1, 2, 3)

            def late():
                n = NZ // 2
                y1, y3 = wrap(y + 1, NY), wrap(y - 1, NY)
                self.got(0)
                p[y1, :n] = p[y1, :n] + one[0]
                self.start(4)
                self.got(1)
                p[y3, n:] = p[y3, n:] + one[1]
                self.start(5)

            def send():
                self.got(2, 3, 4, 5)
                p[y] = p[y] + two[0] + two[1]
                ascending(self, 6)

            def end():
                self.got(*range(6, 6 + NZ - 1))
                total = p[y, z]
                for d in range(NZ - 1):
                    total = total + slots[d]
                finish(self.st, total)

            return [first, late, send, end]

    class D(Stage):
        def copies(self):
            p, two, slots = self.refs
            return [
                lambda d=d: (p.at[wrap(y + d, NY)], two.at[d - 1], dev(dy=d)) for d in range(1, NY)
            ] + last_z(p, slots)

        def program(self):
            p, two, slots = self.refs

            def first():
                def store(v, t):
                    for yy in range(NY):
                        p[yy, :, t] = v[:, yy]

                product(self.st, store)
                self.start(*range(NY - 1))

            def send():
                self.got(*range(NY - 1))
                p[y] = p[y] + two[0] + two[1] + two[2]
                ascending(self, NY - 1)

            def end():
                self.got(*range(NY - 1, NY + NZ - 2))
                total = p[y, z]
                for d in range(NZ - 1):
                    total = total + slots[d]
                finish(self.st, total)

            return [first, send, end]

    class A(Stage):
        def copies(self):
            p, one, two, three, four, slots = self.refs
            lo, hi = pl.ds(0, NY // 2), pl.ds(NY // 2, NY // 2)
            up, down = dev(dz=1), dev(dz=-1)

            def at(d):
                return wrap(z + d, NZ)

            return [
                lambda: (p.at[at(4), lo], one.at[0], up),
                lambda: (p.at[at(4), hi], one.at[1], down),
                lambda: (p.at[at(3), hi], two.at[0, hi], up),
                lambda: (p.at[at(-3), lo], two.at[1, lo], down),
                lambda: (p.at[at(3), lo], two.at[0, lo], up),
                lambda: (p.at[at(-3), hi], two.at[1, hi], down),
                lambda: (p.at[at(2)], three.at[0], up),
                lambda: (p.at[at(-2)], three.at[1], down),
                lambda: (p.at[at(1)], four.at[0], up),
                lambda: (p.at[at(-1)], four.at[1], down),
            ] + [
                lambda d=d: (p.at[z, wrap(y + d, NY)], slots.at[d - 1], dev(dy=d)) for d in range(1, NY)
            ]

        def program(self):
            p, one, two, three, four, slots = self.refs
            n = NY // 2

            def at(d):
                return wrap(z + d, NZ)

            def first():
                def store(v, t):
                    p[:, :, t] = v

                product(self.st, store)
                self.start(0, 1, 2, 3)

            def second():
                self.got(0)
                p[at(3), :n] = p[at(3), :n] + one[0]
                self.start(4)
                self.got(1)
                p[at(-3), n:] = p[at(-3), n:] + one[1]
                self.start(5)

            def third():
                self.got(2, 4)
                p[at(2)] = p[at(2)] + two[0]
                self.start(6)
                self.got(3, 5)
                p[at(-2)] = p[at(-2)] + two[1]
                self.start(7)

            def fourth():
                self.got(6)
                p[at(1)] = p[at(1)] + three[0]
                self.start(8)
                self.got(7)
                p[at(-1)] = p[at(-1)] + three[1]
                self.start(9)

            def send():
                self.got(8, 9)
                p[z] = p[z] + four[0] + four[1]
                self.start(10, 11, 12)

            def end():
                self.got(10, 11, 12)
                finish(self.st, p[z, y] + slots[0] + slots[1] + slots[2])

            return [first, second, third, fourth, send, end]

    stages, used_refs = [], 0
    for st, (kind, _, _, _) in enumerate(STAGES):
        count = len(stage_scratch(STAGES[st]))
        stages.append({"A": A, "B": B, "D": D}[kind](st, bufs[used_refs : used_refs + count]))
        used_refs += count
    gather_step = 1
    for name in PLAN:
        if name == G:
            gather_rest(1, gather_step)
            gather_step += 1
        else:
            stages[name].next()

    for hf in range(HALVES):
        for n in range(len(pieces)):
            piece(hf, n).wait_send()
    for stage in stages:
        stage.sent()


def stage_scratch(stage):
    kind, _, _, nt = stage
    dma = pltpu.SemaphoreType.DMA

    def block(*lead):
        return pltpu.VMEM((*lead, nt, 8, COLS), f32)

    if kind == "A":
        ring = [block(2, NY // 2), block(2, NY), block(2, NY), block(2, NY)]
        return [block(NZ, NY), *ring, block(NY - 1), dma((13,)), dma((13,))]
    if kind == "B":
        return [block(NY, NZ), block(2, NZ // 2), block(2, NZ), block(NZ - 1), dma((13,)), dma((13,))]
    return [block(NY, NZ), block(NY - 1, NZ), block(NZ - 1), dma((10,)), dma((10,))]


def on_device(
    lesser_hist, greater_hist, advanced_hist, current_row, adjacency, weight_table, step_index
):
    vmem, dma, smem = pltpu.VMEM, pltpu.SemaphoreType.DMA, pltpu.SMEM
    lhs = vmem((HALVES, NS, 2, 2, 4, ROWS, COLS), bf16)
    rhs = vmem((NT // 2, NS, 512, 256), bf16)
    scratch = [
        smem((NS,), jnp.int32),
        smem((1,), jnp.int32),
        vmem((2, NS, ROWS, COLS), f32),
        vmem((2, NS, ROWS, COLS), f32),
        vmem((NT, 2, NS, 256, COLS), f32),
        vmem((2, NT, 8, COLS), f32),
        vmem((8, 256), jnp.int32),
        vmem((HALVES, 8, NS, ROWS, COLS), f32),
        lhs, lhs, rhs, rhs,
        vmem((HALVES, 256, 128), bf16),
        vmem((NT // 2, 128, 256), bf16),
        dma((6,)), dma((NT,)), dma((HALVES, 13)), dma((HALVES, 13)),
    ]
    for stage in STAGES:
        scratch += stage_scratch(stage)
    return pl.pallas_call(
        kernel,
        out_shape=jax.ShapeDtypeStruct((2, NT, 8, COLS), f32),
        in_specs=[pl.BlockSpec(memory_space=pl.ANY)] * 7,
        out_specs=pl.BlockSpec(memory_space=vmem),
        scratch_shapes=scratch,
        compiler_params=pltpu.CompilerParams(
            collective_id=0, has_side_effects=True, vmem_limit_bytes=55136 * 1024
        ),
        name="row_step",
    )(
        weight_table, step_index, lesser_hist, jnp.swapaxes(greater_hist, 2, 3), advanced_hist,
        current_row, adjacency,
    )


def solution(mesh):
    in_specs = (
        P(None, "hist", "ocol", "orow"),
        P(None, "hist", "orow", "ocol"),
        P(None, "hist", "ocol", None, "orow"),
        P(None, "ocol", "hist", "orow"),
        P("hist", None),
        P("hist"),
        P(),
    )
    out_specs = P(None, "ocol", "hist", "orow")
    return jax.shard_map(
        on_device, mesh=mesh, in_specs=in_specs, out_specs=out_specs, check_vma=False
    )
```
